32 devices in a mesh: groups: 2 (over x), expert: 16 (over z, y, core).
Axes of the slice: x: 2, y: 2, z: 4, core: 2. Of those that a mesh axis runs over, the one named last changes fastest.
Arguments:
- tokens: bfloat16 [2048, 4096], P(('groups', 'expert')), parts along dimension 0, may hold values from -6 to 6
- routes: int32 [2048, 8], P(('groups', 'expert')), parts along dimension 0, may hold values from 0 to 7, as said below
- route_weights: float32 [2048, 8], P(('groups', 'expert')), parts along dimension 0, may hold values from 0.05 to 0.25
- slot_experts: int32 [8], replicated, may hold values from 0 to 7, each once
- gateup_base: bfloat16 [16, 4096, 768], P('expert'), may hold values from -0.09375 to 0.09375
- down_base: bfloat16 [16, 384, 4096], P('expert'), may hold values from -0.21875 to 0.21875
- entry_factor: bfloat16 [8, 4096, 64], P(None, 'expert'), may hold values from -0.09375 to 0.09375
- gating_factor: bfloat16 [8, 1536, 64], P(None, 'expert'), may hold values from -0.75 to 0.75
- hidden_factor: bfloat16 [8, 768, 64], P(None, 'expert'), may hold values from -0.21875 to 0.21875
- output_factor: bfloat16 [8, 4096, 64], P(None, 'expert'), may hold values from -0.75 to 0.75
Outputs:
- mixed: bfloat16 [2048, 4096], P(('groups', 'expert')), parts along dimension 0
The draws below stay inside these ranges and needn't reach their ends.
There are 2 independent parts, one for each index of `groups`. The reference program is written for one: setup_inputs(seed, part) draws one part's arguments, and reference() takes and returns one part's arrays. A program takes and returns all parts, laid end to end along the dimension named above; an argument that names none is the same for every part. Nothing has to cross between parts.
Inputs may be any that keep to these rules, and one draw needn't show every extreme that they name: `routes`: each row names 8 different experts. Within the rows of one device (aligned blocks of 64 rows) each expert is named at least 64 and at most 64 times, and in every draw one expert is named exactly 64 times within the rows of every device.
All inputs are finite; a program needn't handle non-finite values.
Results may differ from the reference program's by a relative error of at most 0.0062.
Values may be sent and summed in bfloat16 or wider, within the bound.
No kernel may reach another device: no remote copies, remote signals or barrier semaphores. Data moves between devices by JAX's collectives and lax.ppermute only.
A program may use at most 128 MiB of HBM per device.

```python
import jax
import jax.numpy as jnp
from jax import lax

D = 4096
H = 768
R = 64
TOPK = 8
TOK_DEV = 64
EXPERTS = 8
TOKENS = 1024
MEAN = 64
CAP = 64
N_EXPERT = 16


def draw_routes(key, part):
    key = jax.random.fold_in(key, 7)
    spread = CAP - MEAN
    hot_expert = jax.random.randint(jax.random.fold_in(key, 1), (), 0, EXPERTS)

    def one_block(block_key):
        first_key, second_key, third_key, fourth_key = jax.random.split(block_key, 4)
        shuffled = jax.random.permutation(first_key, EXPERTS)
        positions = jnp.arange(EXPERTS)
        first_entry = shuffled[0]
        shuffled = jnp.where(shuffled == hot_expert, first_entry, shuffled)
        shuffled = jnp.where(positions == 0, hot_expert, shuffled)
        moved = jax.random.randint(second_key, (EXPERTS // 2,), 0, spread + 1)
        moved = moved.at[0].set(spread)
        by_position = jnp.stack((MEAN + moved, MEAN - moved), axis=1).reshape(EXPERTS)
        counts = jnp.zeros((EXPERTS,), jnp.int32).at[shuffled].set(by_position.astype(jnp.int32))
        ticket_order = jax.random.permutation(third_key, EXPERTS)
        tickets = jnp.repeat(ticket_order, counts[ticket_order], total_repeat_length=TOK_DEV * TOPK)
        picked_experts = tickets.reshape(TOPK, TOK_DEV).T
        row_order = jax.random.permutation(fourth_key, TOK_DEV)
        return picked_experts[row_order]
    block_keys = jax.random.split(jax.random.fold_in(key, 2), N_EXPERT)
    return jax.vmap(one_block)(block_keys).reshape(TOKENS, TOPK).astype(jnp.int32)


def level_of(rng, extent, pieces, low, high):
    gain, own = 1.0, jax.random.fold_in(rng, 6)
    for position, parts in pieces:
        draws = jnp.exp(jax.random.uniform(jax.random.fold_in(own, position), (parts,), jnp.float32, low / len(pieces), high / len(pieces)))
        gain = gain * jnp.repeat(draws, extent[position] // parts).reshape([-1 if axis == position else 1 for axis in range(len(extent))])
    return gain


def bell_draw(key, dims, deviation, bound, cuts=(), held_as=jnp.bfloat16):
    array = deviation * jax.random.normal(key, dims, jnp.float32)
    if cuts:
        array = array * level_of(key, dims, cuts, -0.22, 0.18)
    return jnp.clip(array, -bound, bound).astype(held_as)


def setup_inputs(seed: int = 0, part: int = 0) -> dict:
    key_of = jax.random.split(jax.random.key(seed), 11)
    part_keys = jax.random.split(jax.random.fold_in(key_of[10], part), 11)
    return {
        "tokens": bell_draw(part_keys[0], (TOKENS, D), 1.0, 6.0, ((0, 16),)),
        "routes": draw_routes(jax.random.fold_in(jax.random.fold_in(key_of[10], part), 71), part),
        "route_weights": jnp.clip(0.05 + 0.2 * jax.random.uniform(part_keys[2], (TOKENS, TOPK), jnp.float32) ** level_of(part_keys[2], (TOKENS, TOPK), ((0, 16),), -0.2, 0.2), 0.05, 0.25),
        "slot_experts": jax.random.permutation(key_of[3], EXPERTS).astype(jnp.int32),
        "gateup_base": bell_draw(key_of[4], (2 * EXPERTS, D, H), D ** -0.5, 0.09375, ((0, 16),)),
        "down_base": bell_draw(key_of[5], (2 * EXPERTS, H // 2, D), H ** -0.5, 0.21875, ((0, 16),)),
        "entry_factor": bell_draw(key_of[6], (EXPERTS, D, R), D ** -0.5, 0.09375, ((1, 16),)),
        "gating_factor": bell_draw(key_of[7], (EXPERTS, 2 * H, R), R ** -0.5, 0.75, ((1, 16),)),
        "hidden_factor": bell_draw(key_of[8], (EXPERTS, H, R), H ** -0.5, 0.21875, ((1, 16),)),
        "output_factor": bell_draw(key_of[9], (EXPERTS, D, R), R ** -0.5, 0.75, ((1, 16),)),
    }


adapter_scale = 0.5


def contracted_rows(left, right):
    return lax.dot_general(left, right, (((1,), (1,)), ((), ())), preferred_element_type=jnp.float32)


def expert_block(row_block, near_gateup, far_gateup, near_down, far_down, entry_rows, gating_rows, hidden_rows, output_matrix_rows, parity):
    width_half = near_gateup.shape[1] // 2
    hidden_width = hidden_rows.shape[0]
    local_start = parity * width_half
    remote_start = (1 - parity) * width_half
    local_product = jnp.dot(row_block, near_gateup, preferred_element_type=jnp.float32)
    remote_product = jnp.dot(row_block, far_gateup, preferred_element_type=jnp.float32)
    rank_rows = jnp.dot(row_block, entry_rows, preferred_element_type=jnp.float32).astype(jnp.bfloat16)
    adapter_gateup = contracted_rows(rank_rows, gating_rows)

    def column_tile_block(begin):
        return lax.dynamic_slice_in_dim(adapter_gateup, begin, width_half, 1)

    local_gate = local_product[:, :width_half] + adapter_scale * column_tile_block(local_start)
    local_up = local_product[:, width_half:] + adapter_scale * column_tile_block(hidden_width + local_start)
    remote_gate = remote_product[:, :width_half] + adapter_scale * column_tile_block(remote_start)
    remote_up = remote_product[:, width_half:] + adapter_scale * column_tile_block(hidden_width + remote_start)
    hidden_near = (jax.nn.silu(local_gate) * local_up).astype(jnp.bfloat16)
    hidden_far = (jax.nn.silu(remote_gate) * remote_up).astype(jnp.bfloat16)
    base_result_rows = jnp.dot(hidden_near, near_down, preferred_element_type=jnp.float32)
    base_result_rows = base_result_rows + jnp.dot(hidden_far, far_down, preferred_element_type=jnp.float32)
    rank_near = lax.dynamic_slice_in_dim(hidden_rows, local_start, width_half, 0)
    rank_far = lax.dynamic_slice_in_dim(hidden_rows, remote_start, width_half, 0)
    adapter_rank = jnp.dot(hidden_near, rank_near, preferred_element_type=jnp.float32)
    adapter_rank = (adapter_rank + jnp.dot(hidden_far, rank_far, preferred_element_type=jnp.float32)).astype(jnp.bfloat16)
    return (base_result_rows + adapter_scale * contracted_rows(adapter_rank, output_matrix_rows)).astype(jnp.bfloat16)


def reference(tokens, routes, route_weights, slot_experts, gateup_base, down_base, entry_factor, gating_factor, hidden_factor, output_factor):
    token_count = tokens.shape[0]
    expert_count = slot_experts.shape[0]
    row_limit = N_EXPERT * CAP
    padded = jnp.concatenate((tokens, jnp.zeros((1, tokens.shape[1]), jnp.bfloat16)), axis=0)
    slot_table = jnp.zeros((expert_count,), jnp.int32).at[slot_experts.astype(jnp.int32)].set(jnp.arange(expert_count, dtype=jnp.int32))

    def expert_step(totals, expert_id):
        matches = routes == expert_id
        row_weight = jnp.sum(jnp.where(matches, route_weights, jnp.float32(0.0)), axis=1)
        row_weight = jnp.concatenate((row_weight, jnp.zeros((1,), row_weight.dtype)), axis=0)
        row_index = jnp.nonzero(jnp.any(matches, axis=1), size=row_limit, fill_value=token_count)[0].astype(jnp.int32)
        pair_slot = slot_table[expert_id].astype(jnp.int32)
        expert_rows = expert_block(
            padded[row_index],
            gateup_base[2 * pair_slot], gateup_base[2 * pair_slot + 1],
            down_base[2 * pair_slot], down_base[2 * pair_slot + 1],
            entry_factor[expert_id], gating_factor[expert_id], hidden_factor[expert_id], output_factor[expert_id], 0)
        weighted = row_weight[row_index][:, None] * expert_rows.astype(jnp.float32)
        return totals.at[row_index].add(weighted), None

    start = jnp.zeros((token_count + 1, tokens.shape[1]), jnp.float32)
    totals, unused = lax.scan(expert_step, start, jnp.arange(expert_count, dtype=jnp.int32))
    return totals[:token_count].astype(jnp.bfloat16)
```

```python
from functools import partial

import jax
import jax.numpy as jnp
from jax import lax
from jax.experimental import pallas as pl
from jax.experimental.pallas import tpu as pltpu
from jax.sharding import PartitionSpec as P

adapter_scale = 0.5


def partner(block, axis, apart):
    count = lax.axis_size(axis)
    route = []
    for low in range(count):
        high = low | 1 << apart
        if high != low and high < count:
            route += [(low, high), (high, low)]
    return lax.ppermute(block, axis, route)


def contracted_rows(left, right):
    return lax.dot_general(
        left, right, (((1,), (1,)), ((), ())), preferred_element_type=jnp.float32
    )


def expert_block(
    row_block,
    near_gateup,
    far_gateup,
    near_down,
    far_down,
    entry_rows,
    gating_rows,
    hidden_rows,
    output_matrix_rows,
    parity,
):
    width_half = near_gateup.shape[1] // 2
    hidden_width = hidden_rows.shape[0]
    local_start = parity * width_half
    remote_start = (1 - parity) * width_half
    local_product = jnp.dot(row_block, near_gateup, preferred_element_type=jnp.float32)
    remote_product = jnp.dot(row_block, far_gateup, preferred_element_type=jnp.float32)
    rank_rows = jnp.dot(row_block, entry_rows, preferred_element_type=jnp.float32).astype(
        jnp.bfloat16
    )
    adapter_gateup = contracted_rows(rank_rows, gating_rows)

    def column_tile_block(begin):
        return lax.dynamic_slice_in_dim(adapter_gateup, begin, width_half, 1)

    local_gate = local_product[:, :width_half] + adapter_scale * column_tile_block(local_start)
    local_up = local_product[:, width_half:] + adapter_scale * column_tile_block(
        hidden_width + local_start
    )
    remote_gate = remote_product[:, :width_half] + adapter_scale * column_tile_block(remote_start)
    remote_up = remote_product[:, width_half:] + adapter_scale * column_tile_block(
        hidden_width + remote_start
    )
    hidden_near = (jax.nn.silu(local_gate) * local_up).astype(jnp.bfloat16)
    hidden_far = (jax.nn.silu(remote_gate) * remote_up).astype(jnp.bfloat16)
    base_result_rows = jnp.dot(hidden_near, near_down, preferred_element_type=jnp.float32)
    base_result_rows = base_result_rows + jnp.dot(
        hidden_far, far_down, preferred_element_type=jnp.float32
    )
    rank_near = lax.dynamic_slice_in_dim(hidden_rows, local_start, width_half, 0)
    rank_far = lax.dynamic_slice_in_dim(hidden_rows, remote_start, width_half, 0)
    adapter_rank = jnp.dot(hidden_near, rank_near, preferred_element_type=jnp.float32)
    adapter_rank = (
        adapter_rank + jnp.dot(hidden_far, rank_far, preferred_element_type=jnp.float32)
    ).astype(jnp.bfloat16)
    return (
        base_result_rows + adapter_scale * contracted_rows(adapter_rank, output_matrix_rows)
    ).astype(jnp.bfloat16)


def unpack_factors(received, model_width, hidden_width):
    devices = received.shape[0]
    width_rows = model_width // devices
    hidden_rows = hidden_width // devices
    entry_rows = received[:, :width_rows].reshape(model_width, -1)
    output_matrix_rows = received[:, width_rows : 2 * width_rows].reshape(model_width, -1)
    gating_rows = received[:, 2 * width_rows : 2 * width_rows + 2 * hidden_rows].reshape(
        2 * hidden_width, -1
    )
    down_rows = received[:, 2 * width_rows + 2 * hidden_rows :].reshape(hidden_width, -1)
    return (entry_rows, gating_rows, down_rows, output_matrix_rows)


def per_device(
    tokens,
    routes,
    route_weights,
    slot_experts,
    gateup_base,
    down_base,
    entry_factor,
    gating_factor,
    hidden_factor,
    output_factor,
):
    devices = lax.axis_size("expert")
    experts = devices // 2
    tok_dev, top_count = routes.shape
    model_width = tokens.shape[1]
    hidden_width = hidden_factor.shape[1] * devices
    mean_load = tok_dev * top_count // experts
    capacity = min(mean_load + 2, tok_dev)
    half_cap = capacity // 2
    stacked = jnp.concatenate((entry_factor, output_factor, gating_factor, hidden_factor), axis=1)
    owner_expert = jnp.repeat(slot_experts, 2)
    factor_send = jnp.take(stacked, owner_expert, axis=0)
    expert_ids = jnp.arange(experts, dtype=jnp.int32)
    slot_table = jnp.sum(
        jnp.where(slot_experts[None, :] == expert_ids[:, None], expert_ids[None, :], 0), axis=1
    )
    flat_routes = routes.reshape(-1)
    one_hot = (flat_routes[:, None] == expert_ids[None, :]).astype(jnp.int32)
    position = jnp.sum(jnp.cumsum(one_hot, axis=0) * one_hot, axis=1) - 1
    pair_slot = jnp.sum(one_hot * slot_table[None, :], axis=1)
    target = (2 * pair_slot + position // half_cap) * half_cap + position % half_cap
    row_ids = jnp.arange(tok_dev * top_count, dtype=jnp.int32) // top_count
    source_row = jnp.full((devices * half_cap,), tok_dev, jnp.int32).at[target].set(row_ids)
    padded = jnp.concatenate((tokens, jnp.zeros((1, model_width), tokens.dtype)), axis=0)
    send_rows = padded[source_row].reshape(devices, half_cap, model_width)
    far_gateup, far_down = partner((gateup_base, down_base), "expert", 0)
    parity = lax.axis_index("expert") % 2
    got_factors = lax.all_to_all(factor_send, "expert", split_axis=0, concat_axis=0, tiled=True)
    factors = unpack_factors(got_factors, model_width, hidden_width)
    pieces = lax.all_to_all(send_rows, "expert", split_axis=0, concat_axis=0, tiled=True)
    entry_rows, gating_rows, down_rows, output_matrix_rows = factors
    outputs = expert_block(
        pieces.reshape(-1, model_width),
        gateup_base[0],
        far_gateup[0],
        down_base[0],
        far_down[0],
        entry_rows,
        gating_rows,
        down_rows,
        output_matrix_rows,
        parity,
    ).reshape(pieces.shape)
    returned = lax.all_to_all(outputs, "expert", split_axis=0, concat_axis=0, tiled=True)
    picked = returned.reshape(devices * half_cap, model_width)[target].reshape(
        tok_dev, top_count, model_width
    )
    result_sum = jnp.zeros((tok_dev, model_width), jnp.float32)
    for column in range(top_count):
        result_sum = result_sum + route_weights[:, column : column + 1] * picked[:, column].astype(
            jnp.float32
        )
    return result_sum.astype(jnp.bfloat16)


f32, bf16 = jnp.float32, jnp.bfloat16
lane_count = 128
chunk_plan = ((1, 2), (3, 4), (5, 6), (7, 0))


def dot(left, right):
    return jnp.dot(left, right, preferred_element_type=f32)


def chunk_kernel(blocks, gate_steps, parity, *refs):
    rows, weights = refs[:blocks], refs[blocks : 2 * blocks]
    near_gateup, far_gateup, near_down, far_down, model_pack = refs[2 * blocks : 2 * blocks + 5]
    near_gate, near_up, far_gate, far_up, near_rank, far_rank = refs[2 * blocks + 5 : 2 * blocks + 11]
    outs = refs[2 * blocks + 11 : 3 * blocks + 11]
    near_total, far_total, rank_total, hidden, low_rank = refs[3 * blocks + 11 :]
    step = pl.program_id(0)
    block_rows = rows[0].shape[0]
    half = hidden.shape[1] // 2
    rank = low_rank.shape[1] // 2
    in_rank = lax.broadcasted_iota(jnp.int32, low_rank.shape, 1) < rank

    @pl.when(step < gate_steps)
    def _():
        tile = jnp.concatenate([ref[...] for ref in rows], axis=0)
        near = dot(tile, near_gateup[0])
        far = dot(tile, far_gateup[0])
        low = dot(tile, model_pack[...])

        @pl.when(step == 0)
        def _():
            near_total[...] = near
            far_total[...] = far
            rank_total[...] = low

        @pl.when(step > 0)
        def _():
            near_total[...] += near
            far_total[...] += far
            rank_total[...] += low

    @pl.when(step == gate_steps - 1)
    def _():
        rank_rows = jnp.where(in_rank, rank_total[...], 0.0).astype(bf16)

        def activate(total, gate_rows, up_rows):
            gate = total[:, :half] + adapter_scale * contracted_rows(rank_rows, gate_rows[0])
            up = total[:, half:] + adapter_scale * contracted_rows(rank_rows, up_rows[0])
            return (gate / (1.0 + jnp.exp(-gate)) * up).astype(bf16)

        hidden_near = activate(near_total, near_gate, near_up)
        hidden_far = activate(far_total, far_gate, far_up)
        hidden[:, :half] = hidden_near
        hidden[:, half:] = hidden_far
        low = dot(hidden_near, near_rank[0]) + dot(hidden_far, far_rank[0])
        low_rank[...] = jnp.where(in_rank, 0.0, low).astype(bf16)

    @pl.when(step >= gate_steps)
    def _():
        result = dot(hidden[:, :half], near_down[0]) + dot(hidden[:, half:], far_down[0])
        result = result + adapter_scale * contracted_rows(low_rank[...], model_pack[...])
        result = result.astype(bf16).astype(f32)
        for index in range(blocks):
            own = result[index * block_rows : (index + 1) * block_rows]
            outs[index][...] = (weights[index][...] * own).astype(bf16)


def expert_chunk(rows, weights, near_gateup, far_gateup, near_down, far_down, factors, parity):
    model_pack, gate_pack, hidden_pack = factors
    blocks = len(rows)
    block_rows, width = rows[0].shape
    both, half = near_gateup.shape[2], near_gateup.shape[2] // 2
    tile = min(1024, width)
    steps = width // tile
    total_rows = blocks * block_rows

    def gate_tile(step):
        return jnp.minimum(step, steps - 1)

    def down_tile(step):
        return jnp.maximum(step - steps, 0)

    row_spec = pl.BlockSpec((block_rows, tile), lambda i, p: (0, gate_tile(i)))
    weight_spec = pl.BlockSpec((block_rows, 1), lambda i, p: (0, 0))
    gateup_spec = pl.BlockSpec((1, tile, both), lambda i, p: (0, gate_tile(i), 0))
    down_spec = pl.BlockSpec((1, half, tile), lambda i, p: (0, 0, down_tile(i)))
    pack_spec = pl.BlockSpec((tile, lane_count), lambda i, p: (jnp.where(i < steps, i, i - steps), 0))
    part_specs = [
        pl.BlockSpec((1, half, lane_count), lambda i, p: (p[0], 0, 0)),
        pl.BlockSpec((1, half, lane_count), lambda i, p: (2 + p[0], 0, 0)),
        pl.BlockSpec((1, half, lane_count), lambda i, p: (1 - p[0], 0, 0)),
        pl.BlockSpec((1, half, lane_count), lambda i, p: (3 - p[0], 0, 0)),
        pl.BlockSpec((1, half, lane_count), lambda i, p: (p[0], 0, 0)),
        pl.BlockSpec((1, half, lane_count), lambda i, p: (1 - p[0], 0, 0)),
    ]
    in_specs = [row_spec] * blocks + [weight_spec] * blocks + [gateup_spec] * 2 + [down_spec] * 2
    out_spec = pl.BlockSpec((block_rows, tile), lambda i, p: (0, down_tile(i)))
    return pl.pallas_call(
        partial(chunk_kernel, blocks, steps),
        out_shape=[jax.ShapeDtypeStruct((block_rows, width), bf16)] * blocks,
        grid_spec=pltpu.PrefetchScalarGridSpec(
            num_scalar_prefetch=1,
            grid=(2 * steps,),
            in_specs=in_specs + [pack_spec] + part_specs,
            out_specs=[out_spec] * blocks,
            scratch_shapes=[
                pltpu.VMEM((total_rows, both), f32),
                pltpu.VMEM((total_rows, both), f32),
                pltpu.VMEM((total_rows, lane_count), f32),
                pltpu.VMEM((total_rows, both), bf16),
                pltpu.VMEM((total_rows, lane_count), bf16),
            ],
        ),
        compiler_params=pltpu.CompilerParams(vmem_limit_bytes=24 * 2**20),
        cost_estimate=pl.CostEstimate(
            flops=2 * total_rows * width * (3 * both + 2 * lane_count),
            bytes_accessed=2 * (3 * both * width + 2 * total_rows * width),
            transcendentals=total_rows * both,
        ),
        name="expert_chunk",
    )(
        parity, *rows, *weights, near_gateup, far_gateup, near_down, far_down, model_pack,
        gate_pack, gate_pack, gate_pack, gate_pack, hidden_pack, hidden_pack,
    )


def ring_order(chips):
    return list(range(0, chips, 2)) + list(range(1, chips, 2))[::-1]


def hop_pairs(order, hops):
    count = len(order)
    pairs = []
    for place in range(count):
        for core, sign in ((0, 1), (1, -1)):
            pairs.append((2 * order[place] + core, 2 * order[(place + sign * hops) % count] + core))
    return pairs


def weight_pieces(weights):
    high = lax.reduce_precision(weights, 8, 7)
    middle = lax.reduce_precision(weights - high, 8, 7)
    return [piece.astype(bf16) for piece in (high, middle, weights - high - middle)]


def dense_per_device(
    tokens, routes, route_weights, slot_experts, gateup_base, down_base,
    entry_factor, gating_factor, hidden_factor, output_factor,
):
    devices = lax.axis_size("expert")
    chips = devices // 2
    tok_dev, width = tokens.shape
    experts, width_rows, rank = entry_factor.shape
    gating_rows, hidden_rows = gating_factor.shape[1], hidden_factor.shape[1]
    order = ring_order(chips)
    pairs = hop_pairs(order, 1)
    me = lax.axis_index("expert")
    parity, chip = me % 2, me // 2
    order_array = jnp.array(order, jnp.int32)
    place = jnp.sum(jnp.where(order_array == chip, jnp.arange(chips, dtype=jnp.int32), 0))
    sign = 1 - 2 * parity
    hops = jnp.arange(chips, dtype=jnp.int32)

    far_gateup, far_down = partner((gateup_base, down_base), "expert", 0)
    rows = [tokens]
    for _ in range(1, chips):
        rows.append(lax.ppermute(rows[-1], "expert", pairs))

    expert_ids = jnp.arange(experts, dtype=jnp.int32)
    named = routes[None, :, :] == expert_ids[:, None, None]
    by_expert = jnp.sum(jnp.where(named, route_weights[None, :, :], 0.0), axis=2)
    pieces = jnp.stack(weight_pieces(by_expert), axis=1)
    spare = jnp.zeros((experts, gating_rows - hidden_rows - 3, rank), bf16)
    right = jnp.concatenate((hidden_factor, pieces, spare), axis=1)
    stacked = jnp.concatenate(
        (
            jnp.concatenate((entry_factor, output_factor), axis=2),
            jnp.concatenate((gating_factor, right), axis=2),
        ),
        axis=1,
    )
    target_chip = order_array[(place + sign * hops) % chips]
    factor_send = jnp.take(stacked, slot_experts[target_chip], axis=0)
    got = [factor_send[0]]
    for hop in range(1, chips):
        got.append(lax.ppermute(factor_send[hop], "expert", hop_pairs(order, hop)))
    got = jnp.stack(got)
    hidden_end = width_rows + hidden_rows
    weights = jnp.sum(got[:, hidden_end : hidden_end + 3, rank:].astype(f32), axis=1)[:, :, None]
    hop_of_chip = (sign * (place - jnp.argsort(order_array))) % chips
    near_pack = jnp.take(got, hop_of_chip, axis=0)
    far_pack = partner(near_pack, "expert", 0)
    even = jnp.where(parity == 0, near_pack, far_pack)
    odd = jnp.where(parity == 0, far_pack, near_pack)
    by_device = jnp.stack((even, odd), axis=1)
    model_pack = by_device[:, :, :width_rows].reshape(width, 2 * rank)
    gate_pack = by_device[:, :, width_rows:].reshape(4, -1, 2 * rank)
    hidden_pack = by_device[:, :, width_rows:hidden_end].reshape(2, -1, 2 * rank)
    factors = (model_pack, gate_pack, hidden_pack)

    outputs = {}
    for members in chunk_plan:
        results = expert_chunk(
            [rows[hop] for hop in members], [weights[hop] for hop in members],
            gateup_base, far_gateup, down_base, far_down, factors, parity.reshape(1),
        )
        outputs.update(zip(members, results))
    running = outputs[1]
    for hop in range(1, chips):
        arrived = lax.ppermute(running, "expert", pairs)
        running = arrived.astype(f32) + outputs[(hop + 1) % chips].astype(f32)
        running = running.astype(bf16)
    return running


def program(*args):
    routes, entry_factor, tokens = args[1], args[6], args[0]
    experts, rank = entry_factor.shape[0], entry_factor.shape[2]
    every = routes.shape[1] == experts and lax.axis_size("expert") == 2 * experts
    every = every and experts == 8 and 2 * rank == lane_count and tokens.shape[0] == rank
    return (dense_per_device if every else per_device)(*args)


def solution(mesh):
    in_specs = (
        P(("groups", "expert"), None),
        P(("groups", "expert"), None),
        P(("groups", "expert"), None),
        P(),
        P("expert", None, None),
        P("expert", None, None),
        P(None, "expert", None),
        P(None, "expert", None),
        P(None, "expert", None),
        P(None, "expert", None),
    )
    out_specs = P(("groups", "expert"), None)
    return jax.shard_map(
        program, mesh=mesh, in_specs=in_specs, out_specs=out_specs, check_vma=False
    )
```

```python
from functools import partial

import jax
import jax.numpy as jnp
from jax import lax
from jax.experimental import pallas as pl
from jax.experimental.pallas import tpu as pltpu
from jax.sharding import PartitionSpec as P

adapter_scale = 0.5


def partner(block, axis, apart):
    count = lax.axis_size(axis)
    route = []
    for low in range(count):
        high = low | 1 << apart
        if high != low and high < count:
            route += [(low, high), (high, low)]
    return lax.ppermute(block, axis, route)


def contracted_rows(left, right):
    return lax.dot_general(
        left, right, (((1,), (1,)), ((), ())), preferred_element_type=jnp.float32
    )


def expert_block(
    row_block,
    near_gateup,
    far_gateup,
    near_down,
    far_down,
    entry_rows,
    gating_rows,
    hidden_rows,
    output_matrix_rows,
    parity,
):
    width_half = near_gateup.shape[1] // 2
    hidden_width = hidden_rows.shape[0]
    local_start = parity * width_half
    remote_start = (1 - parity) * width_half
    local_product = jnp.dot(row_block, near_gateup, preferred_element_type=jnp.float32)
    remote_product = jnp.dot(row_block, far_gateup, preferred_element_type=jnp.float32)
    rank_rows = jnp.dot(row_block, entry_rows, preferred_element_type=jnp.float32).astype(
        jnp.bfloat16
    )
    adapter_gateup = contracted_rows(rank_rows, gating_rows)

    def column_tile_block(begin):
        return lax.dynamic_slice_in_dim(adapter_gateup, begin, width_half, 1)

    local_gate = local_product[:, :width_half] + adapter_scale * column_tile_block(local_start)
    local_up = local_product[:, width_half:] + adapter_scale * column_tile_block(
        hidden_width + local_start
    )
    remote_gate = remote_product[:, :width_half] + adapter_scale * column_tile_block(remote_start)
    remote_up = remote_product[:, width_half:] + adapter_scale * column_tile_block(
        hidden_width + remote_start
    )
    hidden_near = (jax.nn.silu(local_gate) * local_up).astype(jnp.bfloat16)
    hidden_far = (jax.nn.silu(remote_gate) * remote_up).astype(jnp.bfloat16)
    base_result_rows = jnp.dot(hidden_near, near_down, preferred_element_type=jnp.float32)
    base_result_rows = base_result_rows + jnp.dot(
        hidden_far, far_down, preferred_element_type=jnp.float32
    )
    rank_near = lax.dynamic_slice_in_dim(hidden_rows, local_start, width_half, 0)
    rank_far = lax.dynamic_slice_in_dim(hidden_rows, remote_start, width_half, 0)
    adapter_rank = jnp.dot(hidden_near, rank_near, preferred_element_type=jnp.float32)
    adapter_rank = (
        adapter_rank + jnp.dot(hidden_far, rank_far, preferred_element_type=jnp.float32)
    ).astype(jnp.bfloat16)
    return (
        base_result_rows + adapter_scale * contracted_rows(adapter_rank, output_matrix_rows)
    ).astype(jnp.bfloat16)


def unpack_factors(received, model_width, hidden_width):
    devices = received.shape[0]
    width_rows = model_width // devices
    hidden_rows = hidden_width // devices
    entry_rows = received[:, :width_rows].reshape(model_width, -1)
    output_matrix_rows = received[:, width_rows : 2 * width_rows].reshape(model_width, -1)
    gating_rows = received[:, 2 * width_rows : 2 * width_rows + 2 * hidden_rows].reshape(
        2 * hidden_width, -1
    )
    down_rows = received[:, 2 * width_rows + 2 * hidden_rows :].reshape(hidden_width, -1)
    return (entry_rows, gating_rows, down_rows, output_matrix_rows)


def per_device(
    tokens,
    routes,
    route_weights,
    slot_experts,
    gateup_base,
    down_base,
    entry_factor,
    gating_factor,
    hidden_factor,
    output_factor,
):
    devices = lax.axis_size("expert")
    experts = devices // 2
    tok_dev, top_count = routes.shape
    model_width = tokens.shape[1]
    hidden_width = hidden_factor.shape[1] * devices
    mean_load = tok_dev * top_count // experts
    capacity = min(mean_load + 2, tok_dev)
    half_cap = capacity // 2
    stacked = jnp.concatenate((entry_factor, output_factor, gating_factor, hidden_factor), axis=1)
    owner_expert = jnp.repeat(slot_experts, 2)
    factor_send = jnp.take(stacked, owner_expert, axis=0)
    expert_ids = jnp.arange(experts, dtype=jnp.int32)
    slot_table = jnp.sum(
        jnp.where(slot_experts[None, :] == expert_ids[:, None], expert_ids[None, :], 0), axis=1
    )
    flat_routes = routes.reshape(-1)
    one_hot = (flat_routes[:, None] == expert_ids[None, :]).astype(jnp.int32)
    position = jnp.sum(jnp.cumsum(one_hot, axis=0) * one_hot, axis=1) - 1
    pair_slot = jnp.sum(one_hot * slot_table[None, :], axis=1)
    target = (2 * pair_slot + position // half_cap) * half_cap + position % half_cap
    row_ids = jnp.arange(tok_dev * top_count, dtype=jnp.int32) // top_count
    source_row = jnp.full((devices * half_cap,), tok_dev, jnp.int32).at[target].set(row_ids)
    padded = jnp.concatenate((tokens, jnp.zeros((1, model_width), tokens.dtype)), axis=0)
    send_rows = padded[source_row].reshape(devices, half_cap, model_width)
    far_gateup, far_down = partner((gateup_base, down_base), "expert", 0)
    parity = lax.axis_index("expert") % 2
    got_factors = lax.all_to_all(factor_send, "expert", split_axis=0, concat_axis=0, tiled=True)
    factors = unpack_factors(got_factors, model_width, hidden_width)
    pieces = lax.all_to_all(send_rows, "expert", split_axis=0, concat_axis=0, tiled=True)
    entry_rows, gating_rows, down_rows, output_matrix_rows = factors
    outputs = expert_block(
        pieces.reshape(-1, model_width),
        gateup_base[0],
        far_gateup[0],
        down_base[0],
        far_down[0],
        entry_rows,
        gating_rows,
        down_rows,
        output_matrix_rows,
        parity,
    ).reshape(pieces.shape)
    returned = lax.all_to_all(outputs, "expert", split_axis=0, concat_axis=0, tiled=True)
    picked = returned.reshape(devices * half_cap, model_width)[target].reshape(
        tok_dev, top_count, model_width
    )
    result_sum = jnp.zeros((tok_dev, model_width), jnp.float32)
    for column in range(top_count):
        result_sum = result_sum + route_weights[:, column : column + 1] * picked[:, column].astype(
            jnp.float32
        )
    return result_sum.astype(jnp.bfloat16)


f32, bf16 = jnp.float32, jnp.bfloat16
in_vmem = pl.BlockSpec(memory_space=pltpu.VMEM)
in_smem = pl.BlockSpec(memory_space=pltpu.SMEM)
weight_terms, lane_count, sum_parts = 3, 128, 2
chunk_plan = {0: (1, 2), 1: (3, 7), 2: (4, 5), 4: (6, 0)}


def dot(left, right):
    return jnp.dot(left, right, preferred_element_type=f32)


def ring_order(chips):
    return list(range(0, chips, 2)) + list(range(1, chips, 2))[::-1]


def hop_pairs(order, hops):
    count = len(order)
    pairs = []
    for place in range(count):
        for core, sign in ((0, 1), (1, -1)):
            pairs.append((2 * order[place] + core, 2 * order[(place + sign * hops) % count] + core))
    return pairs


def chip_at_hop(me, hop, chips):
    chip, parity = me // 2, me % 2
    place = jnp.where(chip % 2 == 0, chip // 2, chips - 1 - chip // 2)
    there = (place + (1 - 2 * parity) * hop + chips) % chips
    return jnp.where(there < chips // 2, 2 * there, 2 * (chips - 1 - there) + 1)


def hop_of_send(group, send, chips):
    return jnp.where(group == 0, send, chips - send)


def pack_kernel(chips, ids, slots, entry, output, gating, hidden, *refs):
    me, group = ids[0], ids[1]
    rank, width_rows = entry.shape[1:]
    gating_rows, hidden_rows = gating.shape[2], hidden.shape[1]
    outs, scratch = refs[:-1], refs[-1]
    for send, target in enumerate(outs):
        out = target if send < len(outs) - 1 else scratch
        expert = slots[chip_at_hop(me, hop_of_send(group, send, chips), chips)]
        out[:width_rows, :rank] = entry[expert].T
        out[:width_rows, rank:] = output[expert].T
        out[width_rows:, :rank] = gating[expert].T
        out[width_rows : width_rows + hidden_rows, rank:] = hidden[expert]
        out[width_rows + hidden_rows :, rank:] = jnp.zeros((gating_rows - hidden_rows, rank), bf16)
    size = outs[-1].shape[0]
    outs[-1][...] = scratch[pl.ds(pl.multiple_of(group * size, 16), size)]


def extend_kernel(experts, tokens, routes, weights, out):
    width = tokens.shape[1]
    out[:, :width] = tokens[...]
    left = jnp.concatenate(
        [
            jnp.sum(jnp.where(routes[...] == expert, weights[...], 0.0), axis=0, keepdims=True)
            for expert in range(experts)
        ],
        axis=0,
    )
    terms = []
    for _ in range(weight_terms):
        terms.append(left.astype(bf16).astype(f32))
        left = left - terms[-1]
    terms.append(jnp.zeros((lane_count - weight_terms * experts, left.shape[1]), f32))
    out[:, width:] = jnp.concatenate(terms, axis=0).T.astype(bf16)


def join_kernel(*refs):
    begin = 0
    for source in refs[:-1]:
        refs[-1][begin : begin + source.shape[0]] = source[...]
        begin += source.shape[0]


def collect_kernel(chips, ids, own, mine, twins, near_pack):
    me, group = ids[0], ids[1]
    size = own.shape[0]
    near_pack[chip_at_hop(me, 0, chips)] = own[...]
    for source, side in ((mine, group), (twins, 1 - group)):
        for send in range(1, chips // 2):
            chip = chip_at_hop(me, -hop_of_send(side, send, chips), chips)
            near_pack[chip] = source[(send - 1) * size : send * size]
        chip = chip_at_hop(me, -(chips // 2), chips)
        half = pl.ds(pl.multiple_of(side * (size // 2), 16), size // 2)
        near_pack[chip, half] = source[(chips // 2 - 1) * size :]


def load_kernel(parts, *refs):
    sources, targets, ready, done = refs[:2], refs[2:4], refs[4], refs[5]
    copies = []
    for index, (source, target) in enumerate(zip(sources, targets)):
        size = source.shape[1] // parts
        for part in range(parts):
            piece = pl.ds(part * size, size)
            copy = pltpu.make_async_copy(
                source.at[:, piece], target.at[:, piece], done.at[index * parts + part]
            )
            copy.start()
            copies.append(copy)
    for copy in copies:
        copy.wait()
    ready[...] = jnp.zeros_like(ready)


def load_base(gateup, down, parts=4):
    return pl.pallas_call(
        partial(load_kernel, parts),
        out_shape=[pltpu.VMEM(part.shape, part.dtype) for part in (gateup, down)]
        + [jax.ShapeDtypeStruct((8, lane_count), f32)],
        in_specs=[pl.BlockSpec(memory_space=pltpu.HBM)] * 2,
        out_specs=[in_vmem] * 3,
        scratch_shapes=[pltpu.SemaphoreType.DMA((2 * parts,))],
        compiler_params=pltpu.CompilerParams(vmem_limit_bytes=16 * 2**20),
        name="load_base",
    )(*[pltpu.with_memory_space_constraint(part, pltpu.HBM) for part in (gateup, down)])


def chunk_kernel(blocks, chips, ids, slots, *refs):
    arrived = refs[:blocks]
    near_gateup, far_gateup, near_down, far_down, near_pack, far_pack = refs[blocks : blocks + 6]
    outs, (rows, total, hidden) = refs[blocks + 6 : -3], refs[-3:]
    parts = len(outs) // blocks
    me = ids[0]
    parity = me % 2
    block_rows, width = arrived[0].shape[0], near_gateup.shape[1]
    half = near_down.shape[1]
    rank = near_pack.shape[2] // 2
    width_rows = width // (2 * chips)
    gating_rows = near_pack.shape[1] - width_rows
    hidden_rows = gating_rows // 2
    in_rank = lax.broadcasted_iota(jnp.int32, (blocks * block_rows, 2 * rank), 1) < rank

    def pack(chip, core, begin, count):
        part = pl.ds(begin, count)
        return jnp.where(parity == core, near_pack[chip, part], far_pack[chip, part])

    for index in range(blocks):
        rows[index * block_rows : (index + 1) * block_rows] = arrived[index][:, :width]
    total[0] = dot(rows[...], near_gateup[0])
    total[1] = dot(rows[...], far_gateup[0])
    low = jnp.zeros((blocks * block_rows, 2 * rank), f32)
    for chip in range(chips):
        for core in range(2):
            begin = (2 * chip + core) * width_rows
            low = low + dot(rows[:, begin : begin + width_rows], pack(chip, core, 0, width_rows))
    rank_rows = jnp.where(in_rank, low, 0.0).astype(bf16)

    def adapter(first, part, count):
        pieces = [pack(first + device // 2, device % 2, part, count) for device in range(chips // 2)]
        return jnp.concatenate(pieces, axis=0)

    low = None
    for far in range(2):
        which = parity if far == 0 else 1 - parity
        gate_rows = adapter(which * (chips // 4), width_rows, gating_rows)
        up_rows = adapter(chips // 2 + which * (chips // 4), width_rows, gating_rows)
        gate = total[far, :, :half] + adapter_scale * contracted_rows(rank_rows, gate_rows)
        up = total[far, :, half:] + adapter_scale * contracted_rows(rank_rows, up_rows)
        active = (gate / (1.0 + jnp.exp(-gate)) * up).astype(bf16)
        hidden[:, far * half : (far + 1) * half] = active
        pieces = [
            pack(which * (chips // 2) + device // 2, device % 2, width_rows, hidden_rows)
            for device in range(chips)
        ]
        part = dot(active, jnp.concatenate(pieces, axis=0))
        low = part if low is None else low + part
    low_rank = jnp.where(in_rank, 0.0, low).astype(bf16)

    scales = []
    lane = lax.broadcasted_iota(jnp.int32, (block_rows, lane_count), 1)
    ours = (lane % chips == slots[me // 2]) & (lane < weight_terms * chips)
    for source in arrived:
        terms = jnp.where(ours, source[:, width:].astype(f32), 0.0)
        scales.append(jnp.sum(terms, axis=1, keepdims=True))

    for chip in range(chips):
        for core in range(2):
            begin = (2 * chip + core) * width_rows
            columns = slice(begin, begin + width_rows)
            result = dot(hidden[:, :half], near_down[0, :, columns])
            result = result + dot(hidden[:, half:], far_down[0, :, columns])
            result = result + adapter_scale * contracted_rows(low_rank, pack(chip, core, 0, width_rows))
            result = result.astype(bf16).astype(f32)
            for index in range(blocks):
                own = result[index * block_rows : (index + 1) * block_rows]
                part, first = divmod(begin, width // parts)
                out = outs[index * parts + part]
                out[:, first : first + width_rows] = (scales[index] * own).astype(bf16)


def expert_chunk(ids, slots, rows, base, packs, parts):
    blocks = len(rows)
    block_rows, width, both = rows[0].shape[0], base[0].shape[1], base[0].shape[2]
    chips = packs[0].shape[0]
    total_rows = blocks * block_rows
    return pl.pallas_call(
        partial(chunk_kernel, blocks, chips),
        out_shape=[jax.ShapeDtypeStruct((block_rows, width // parts), bf16)] * (blocks * parts),
        in_specs=[in_smem] * 2 + [in_vmem] * (blocks + 6),
        out_specs=[in_vmem] * (blocks * parts),
        scratch_shapes=[
            pltpu.VMEM((total_rows, width), bf16),
            pltpu.VMEM((2, total_rows, both), f32),
            pltpu.VMEM((total_rows, both), bf16),
        ],
        compiler_params=pltpu.CompilerParams(vmem_limit_bytes=16 * 2**20),
        cost_estimate=pl.CostEstimate(flops=2**16, bytes_accessed=2**16, transcendentals=0),
        name="expert_chunk",
    )(ids, slots, *rows, *base, *packs)


def dense_per_device(
    tokens, routes, route_weights, slot_experts, gateup_base, down_base,
    entry_factor, gating_factor, hidden_factor, output_factor,
):
    chips = lax.axis_size("expert") // 2
    width_rows, rank = entry_factor.shape[1:]
    gating_rows = gating_factor.shape[1]
    order = ring_order(chips)
    size = width_rows + gating_rows
    me = lax.axis_index("expert").astype(jnp.int32)
    ids = jnp.stack((me, lax.axis_index("groups").astype(jnp.int32)))
    devices = 2 * chips

    def keep(array):
        return pltpu.with_memory_space_constraint(array, pltpu.VMEM)

    def ahead(block):
        return lax.ppermute(block, "expert", hop_pairs(order, 1))

    def back(block):
        return lax.ppermute(block, "expert", hop_pairs(order, -1))

    def send_factors(block, send):
        pairs = hop_pairs(order, send)
        pairs += [(devices + here, devices + there) for here, there in hop_pairs(order, -send)]
        return lax.ppermute(block, ("groups", "expert"), pairs)

    sends = chips // 2 + 1
    shapes = [jax.ShapeDtypeStruct((size, 2 * rank), bf16)] * (sends - 1)
    shapes.append(jax.ShapeDtypeStruct((size // 2, 2 * rank), bf16))
    packed = pl.pallas_call(
        partial(pack_kernel, chips),
        out_shape=shapes,
        in_specs=[in_smem] * 2 + [in_vmem] * 4,
        out_specs=[in_vmem] * sends,
        scratch_shapes=[pltpu.VMEM((size, 2 * rank), bf16)],
        name="pack_factors",
    )(
        ids, slot_experts,
        jnp.swapaxes(entry_factor, 1, 2), jnp.swapaxes(output_factor, 1, 2),
        jnp.swapaxes(gating_factor, 1, 2), hidden_factor,
    )
    tokens, packed = lax.optimization_barrier((tokens, packed))
    tokens = pl.pallas_call(
        partial(extend_kernel, chips),
        out_shape=jax.ShapeDtypeStruct((tokens.shape[0], tokens.shape[1] + lane_count), bf16),
        in_specs=[in_vmem] * 3,
        out_specs=in_vmem,
        name="extend_tokens",
    )(tokens, routes.T, route_weights.T)
    rows = {0: tokens, 1: ahead(tokens)}
    got = [send_factors(packed[send], send) for send in range(1, sends)]

    rows[1], got, gateup, down = lax.optimization_barrier((rows[1], got, gateup_base, down_base))
    mine = pl.pallas_call(
        join_kernel,
        out_shape=jax.ShapeDtypeStruct((sum(part.shape[0] for part in got), 2 * rank), bf16),
        in_specs=[in_vmem] * (sends - 1),
        out_specs=in_vmem,
        name="join_factors",
    )(*got)
    twins = lax.ppermute(mine, "groups", [(0, 1), (1, 0)])
    rows[7] = back(tokens)
    rows[2] = ahead(rows[1])
    far_gateup = partner(gateup, "expert", 0)
    near_gateup, near_down, ready = load_base(gateup, down)

    twins, rows[2], rows[7], ready, down = lax.optimization_barrier((twins, rows[2], rows[7], ready, down_base))
    near_pack = pl.pallas_call(
        partial(collect_kernel, chips),
        out_shape=jax.ShapeDtypeStruct((chips, size, 2 * rank), bf16),
        in_specs=[in_smem] + [in_vmem] * 3,
        out_specs=in_vmem,
        name="order_factors",
    )(ids, packed[0], mine, twins)
    far_pack = partner(near_pack, "expert", 0)
    far_down = partner(down, "expert", 0)
    base = (near_gateup, keep(far_gateup), near_down, keep(far_down))
    packs = [keep(near_pack), keep(far_pack)]
    rows[6] = back(rows[7])
    rows[3] = ahead(rows[2])
    rows[5] = back(rows[6])
    rows[4] = ahead(rows[3])
    terms = {}

    def compute(members, after):
        blocks = [rows[hop] for hop in members]
        if after is not None:
            blocks, after = lax.optimization_barrier((blocks, after))
        results = expert_chunk(ids, slot_experts, blocks, base, packs, sum_parts)
        for index, hop in enumerate(members):
            terms[hop] = list(results[index * sum_parts : (index + 1) * sum_parts])
        return after

    compute(chunk_plan[0], None)
    running = terms[1]
    for hop in range(2, chips + 1):
        if hop == 2:
            running[-1] = compute(chunk_plan[1], running[-1])
        running = [ahead(part) for part in running]
        if hop in chunk_plan:
            running[-1] = compute(chunk_plan[hop], running[-1])
        running = [
            (part.astype(f32) + term.astype(f32)).astype(bf16)
            for part, term in zip(running, terms[hop % chips])
        ]
    return jnp.concatenate(running, axis=1)


def program(*args):
    routes, entry_factor, tokens = args[1], args[6], args[0]
    experts, rank = entry_factor.shape[0], entry_factor.shape[2]
    every = routes.shape[1] == experts and lax.axis_size("expert") == 2 * experts
    every = every and lax.axis_size("groups") == 2 and experts == 8 and rank == 64 and tokens.shape[0] == rank
    return (dense_per_device if every else per_device)(*args)


def solution(mesh):
    in_specs = (
        P(("groups", "expert"), None),
        P(("groups", "expert"), None),
        P(("groups", "expert"), None),
        P(),
        P("expert", None, None),
        P("expert", None, None),
        P(None, "expert", None),
        P(None, "expert", None),
        P(None, "expert", None),
        P(None, "expert", None),
    )
    out_specs = P(("groups", "expert"), None)
    return jax.shard_map(
        program, mesh=mesh, in_specs=in_specs, out_specs=out_specs, check_vma=False
    )
```

```python
from functools import partial

import jax
import jax.numpy as jnp
from jax import lax
from jax.experimental import pallas as pl
from jax.experimental.pallas import tpu as pltpu
from jax.sharding import PartitionSpec as P

adapter_scale = 0.5


def partner(block, axis, apart):
    count = lax.axis_size(axis)
    route = []
    for low in range(count):
        high = low | 1 << apart
        if high != low and high < count:
            route += [(low, high), (high, low)]
    return lax.ppermute(block, axis, route)


def contracted_rows(left, right):
    return lax.dot_general(
        left, right, (((1,), (1,)), ((), ())), preferred_element_type=jnp.float32
    )


def expert_block(
    row_block,
    near_gateup,
    far_gateup,
    near_down,
    far_down,
    entry_rows,
    gating_rows,
    hidden_rows,
    output_matrix_rows,
    parity,
):
    width_half = near_gateup.shape[1] // 2
    hidden_width = hidden_rows.shape[0]
    local_start = parity * width_half
    remote_start = (1 - parity) * width_half
    local_product = jnp.dot(row_block, near_gateup, preferred_element_type=jnp.float32)
    remote_product = jnp.dot(row_block, far_gateup, preferred_element_type=jnp.float32)
    rank_rows = jnp.dot(row_block, entry_rows, preferred_element_type=jnp.float32).astype(
        jnp.bfloat16
    )
    adapter_gateup = contracted_rows(rank_rows, gating_rows)

    def column_tile_block(begin):
        return lax.dynamic_slice_in_dim(adapter_gateup, begin, width_half, 1)

    local_gate = local_product[:, :width_half] + adapter_scale * column_tile_block(local_start)
    local_up = local_product[:, width_half:] + adapter_scale * column_tile_block(
        hidden_width + local_start
    )
    remote_gate = remote_product[:, :width_half] + adapter_scale * column_tile_block(remote_start)
    remote_up = remote_product[:, width_half:] + adapter_scale * column_tile_block(
        hidden_width + remote_start
    )
    hidden_near = (jax.nn.silu(local_gate) * local_up).astype(jnp.bfloat16)
    hidden_far = (jax.nn.silu(remote_gate) * remote_up).astype(jnp.bfloat16)
    base_result_rows = jnp.dot(hidden_near, near_down, preferred_element_type=jnp.float32)
    base_result_rows = base_result_rows + jnp.dot(
        hidden_far, far_down, preferred_element_type=jnp.float32
    )
    rank_near = lax.dynamic_slice_in_dim(hidden_rows, local_start, width_half, 0)
    rank_far = lax.dynamic_slice_in_dim(hidden_rows, remote_start, width_half, 0)
    adapter_rank = jnp.dot(hidden_near, rank_near, preferred_element_type=jnp.float32)
    adapter_rank = (
        adapter_rank + jnp.dot(hidden_far, rank_far, preferred_element_type=jnp.float32)
    ).astype(jnp.bfloat16)
    return (
        base_result_rows + adapter_scale * contracted_rows(adapter_rank, output_matrix_rows)
    ).astype(jnp.bfloat16)


def unpack_factors(received, model_width, hidden_width):
    devices = received.shape[0]
    width_rows = model_width // devices
    hidden_rows = hidden_width // devices
    entry_rows = received[:, :width_rows].reshape(model_width, -1)
    output_matrix_rows = received[:, width_rows : 2 * width_rows].reshape(model_width, -1)
    gating_rows = received[:, 2 * width_rows : 2 * width_rows + 2 * hidden_rows].reshape(
        2 * hidden_width, -1
    )
    down_rows = received[:, 2 * width_rows + 2 * hidden_rows :].reshape(hidden_width, -1)
    return (entry_rows, gating_rows, down_rows, output_matrix_rows)


def per_device(
    tokens,
    routes,
    route_weights,
    slot_experts,
    gateup_base,
    down_base,
    entry_factor,
    gating_factor,
    hidden_factor,
    output_factor,
):
    devices = lax.axis_size("expert")
    experts = devices // 2
    tok_dev, top_count = routes.shape
    model_width = tokens.shape[1]
    hidden_width = hidden_factor.shape[1] * devices
    mean_load = tok_dev * top_count // experts
    capacity = min(mean_load + 2, tok_dev)
    half_cap = capacity // 2
    stacked = jnp.concatenate((entry_factor, output_factor, gating_factor, hidden_factor), axis=1)
    owner_expert = jnp.repeat(slot_experts, 2)
    factor_send = jnp.take(stacked, owner_expert, axis=0)
    expert_ids = jnp.arange(experts, dtype=jnp.int32)
    slot_table = jnp.sum(
        jnp.where(slot_experts[None, :] == expert_ids[:, None], expert_ids[None, :], 0), axis=1
    )
    flat_routes = routes.reshape(-1)
    one_hot = (flat_routes[:, None] == expert_ids[None, :]).astype(jnp.int32)
    position = jnp.sum(jnp.cumsum(one_hot, axis=0) * one_hot, axis=1) - 1
    pair_slot = jnp.sum(one_hot * slot_table[None, :], axis=1)
    target = (2 * pair_slot + position // half_cap) * half_cap + position % half_cap
    row_ids = jnp.arange(tok_dev * top_count, dtype=jnp.int32) // top_count
    source_row = jnp.full((devices * half_cap,), tok_dev, jnp.int32).at[target].set(row_ids)
    padded = jnp.concatenate((tokens, jnp.zeros((1, model_width), tokens.dtype)), axis=0)
    send_rows = padded[source_row].reshape(devices, half_cap, model_width)
    far_gateup, far_down = partner((gateup_base, down_base), "expert", 0)
    parity = lax.axis_index("expert") % 2
    got_factors = lax.all_to_all(factor_send, "expert", split_axis=0, concat_axis=0, tiled=True)
    factors = unpack_factors(got_factors, model_width, hidden_width)
    pieces = lax.all_to_all(send_rows, "expert", split_axis=0, concat_axis=0, tiled=True)
    entry_rows, gating_rows, down_rows, output_matrix_rows = factors
    outputs = expert_block(
        pieces.reshape(-1, model_width),
        gateup_base[0],
        far_gateup[0],
        down_base[0],
        far_down[0],
        entry_rows,
        gating_rows,
        down_rows,
        output_matrix_rows,
        parity,
    ).reshape(pieces.shape)
    returned = lax.all_to_all(outputs, "expert", split_axis=0, concat_axis=0, tiled=True)
    picked = returned.reshape(devices * half_cap, model_width)[target].reshape(
        tok_dev, top_count, model_width
    )
    result_sum = jnp.zeros((tok_dev, model_width), jnp.float32)
    for column in range(top_count):
        result_sum = result_sum + route_weights[:, column : column + 1] * picked[:, column].astype(
            jnp.float32
        )
    return result_sum.astype(jnp.bfloat16)


f32, bf16 = jnp.float32, jnp.bfloat16
in_vmem = pl.BlockSpec(memory_space=pltpu.VMEM)
in_smem = pl.BlockSpec(memory_space=pltpu.SMEM)
weight_terms, lane_count, sum_parts = 3, 128, 2
small_cost = pl.CostEstimate(flops=2**16, bytes_accessed=2**16, transcendentals=0)
chunk_plan = ((1, 2), (3, 7))
begin_plan, end_plan = {2: (4, 5), 4: (6, 0)}, {3: (4, 5), 5: (6, 0)}


def dot(left, right):
    return jnp.dot(left, right, preferred_element_type=f32)


def ring_order(chips):
    return list(range(0, chips, 2)) + list(range(1, chips, 2))[::-1]


def hop_pairs(order, hops):
    count = len(order)
    pairs = []
    for place in range(count):
        for core, sign in ((0, 1), (1, -1)):
            pairs.append((2 * order[place] + core, 2 * order[(place + sign * hops) % count] + core))
    return pairs


def chip_at_hop(me, hop, chips):
    chip, parity = me // 2, me % 2
    place = jnp.where(chip % 2 == 0, chip // 2, chips - 1 - chip // 2)
    there = (place + (1 - 2 * parity) * hop + chips) % chips
    return jnp.where(there < chips // 2, 2 * there, 2 * (chips - 1 - there) + 1)


def hop_of_send(group, send, chips):
    return jnp.where(group == 0, send, chips - send)


def pack_kernel(chips, slots, tokens, routes, weights, entry, output, gating, hidden, extended, *refs):
    me, group = lax.axis_index("expert"), lax.axis_index("groups")
    extend(chips, tokens, routes, weights, extended)
    rank, width_rows = entry.shape[1:]
    gating_rows, hidden_rows = gating.shape[2], hidden.shape[1]
    outs, scratch = refs[:-1], refs[-1]
    for send, target in enumerate(outs):
        out = target if send < len(outs) - 1 else scratch
        expert = slots[chip_at_hop(me, hop_of_send(group, send, chips), chips)]
        out[:width_rows, :rank] = entry[expert].T
        out[:width_rows, rank:] = output[expert].T
        out[width_rows:, :rank] = gating[expert].T
        out[width_rows : width_rows + hidden_rows, rank:] = hidden[expert]
        out[width_rows + hidden_rows :, rank:] = jnp.zeros((gating_rows - hidden_rows, rank), bf16)
    size = outs[-1].shape[0]
    outs[-1][...] = scratch[pl.ds(pl.multiple_of(group * size, 16), size)]


def extend(experts, tokens, routes, weights, out):
    width = tokens.shape[1]
    out[:, :width] = tokens[...]
    left = jnp.concatenate(
        [
            jnp.sum(jnp.where(routes[...] == expert, weights[...], 0.0), axis=0, keepdims=True)
            for expert in range(experts)
        ],
        axis=0,
    )
    terms = []
    for _ in range(weight_terms):
        terms.append(left.astype(bf16).astype(f32))
        left = left - terms[-1]
    terms.append(jnp.zeros((lane_count - weight_terms * experts, left.shape[1]), f32))
    out[:, width:] = jnp.concatenate(terms, axis=0).T.astype(bf16)


def join_kernel(*refs):
    begin = 0
    for source in refs[:-1]:
        refs[-1][begin : begin + source.shape[0]] = source[...]
        begin += source.shape[0]


def collect_kernel(chips, own, mine, twins, loaded, near_pack):
    del loaded
    me, group = lax.axis_index("expert"), lax.axis_index("groups")
    size = own.shape[0]
    near_pack[chip_at_hop(me, 0, chips)] = own[...]
    for source, side in ((mine, group), (twins, 1 - group)):
        for send in range(1, chips // 2):
            chip = chip_at_hop(me, -hop_of_send(side, send, chips), chips)
            near_pack[chip] = source[(send - 1) * size : send * size]
        chip = chip_at_hop(me, -(chips // 2), chips)
        half = pl.ds(pl.multiple_of(side * (size // 2), 16), size // 2)
        near_pack[chip, half] = source[(chips // 2 - 1) * size :]


def load_kernel(parts, *refs):
    sources, targets, ready, done = refs[:2], refs[2:4], refs[4], refs[5]
    copies = []
    for index, (source, target) in enumerate(zip(sources, targets)):
        size = source.shape[1] // parts
        for part in range(parts):
            piece = pl.ds(part * size, size)
            copy = pltpu.make_async_copy(
                source.at[:, piece], target.at[:, piece], done.at[index * parts + part]
            )
            copy.start()
            copies.append(copy)
    for copy in copies:
        copy.wait()
    ready[...] = jnp.zeros_like(ready)


def load_base(gateup, down, parts=4):
    return pl.pallas_call(
        partial(load_kernel, parts),
        out_shape=[pltpu.VMEM(part.shape, part.dtype) for part in (gateup, down)]
        + [jax.ShapeDtypeStruct((8, lane_count), f32)],
        in_specs=[pl.BlockSpec(memory_space=pltpu.HBM)] * 2,
        out_specs=[in_vmem] * 3,
        scratch_shapes=[pltpu.SemaphoreType.DMA((2 * parts,))],
        compiler_params=pltpu.CompilerParams(vmem_limit_bytes=2**20),
        cost_estimate=small_cost,
        name="load_base",
    )(*[pltpu.with_memory_space_constraint(part, pltpu.HBM) for part in (gateup, down)])


def base_kernel(*refs):
    near_gateup, far_gateup, total, rows = refs[-4:]
    arrived = refs[:-4]
    block_rows, width = arrived[0].shape[0], rows.shape[1]
    for index, source in enumerate(arrived):
        rows[index * block_rows : (index + 1) * block_rows] = source[:, :width]
    total[0] = dot(rows[...], near_gateup[0])
    total[1] = dot(rows[...], far_gateup[0])


def base_chunk(rows, near_gateup, far_gateup):
    blocks, block_rows = len(rows), rows[0].shape[0]
    width, both = near_gateup.shape[1:]
    return pl.pallas_call(
        base_kernel,
        out_shape=pltpu.VMEM((2, blocks * block_rows, both), f32),
        in_specs=[in_vmem] * (blocks + 2),
        out_specs=in_vmem,
        scratch_shapes=[pltpu.VMEM((blocks * block_rows, width), bf16)],
        compiler_params=pltpu.CompilerParams(vmem_limit_bytes=8 * 2**20),
        cost_estimate=small_cost,
        name="base_chunk",
    )(*rows, near_gateup, far_gateup)


def rest_kernel(blocks, chips, slots, *refs):
    me = lax.axis_index("expert")
    arrived = refs[:blocks]
    total, near_down, far_down, near_pack, far_pack = refs[blocks : blocks + 5]
    outs, (rows, hidden) = refs[blocks + 5 : -2], refs[-2:]
    parts = len(outs) // blocks
    parity = me % 2
    block_rows, width = arrived[0].shape[0], rows.shape[1]
    half = near_down.shape[1]
    rank = near_pack.shape[2] // 2
    width_rows = width // (2 * chips)
    gating_rows = near_pack.shape[1] - width_rows
    hidden_rows = gating_rows // 2
    in_rank = lax.broadcasted_iota(jnp.int32, (blocks * block_rows, 2 * rank), 1) < rank

    def pack(chip, core, begin, count):
        part = pl.ds(begin, count)
        return jnp.where(parity == core, near_pack[chip, part], far_pack[chip, part])

    for index in range(blocks):
        rows[index * block_rows : (index + 1) * block_rows] = arrived[index][:, :width]
    low = jnp.zeros((blocks * block_rows, 2 * rank), f32)
    for chip in range(chips):
        for core in range(2):
            begin = (2 * chip + core) * width_rows
            low = low + dot(rows[:, begin : begin + width_rows], pack(chip, core, 0, width_rows))
    rank_rows = jnp.where(in_rank, low, 0.0).astype(bf16)

    def adapter(first, part, count):
        pieces = [pack(first + device // 2, device % 2, part, count) for device in range(chips // 2)]
        return jnp.concatenate(pieces, axis=0)

    low = None
    for far in range(2):
        which = parity if far == 0 else 1 - parity
        gate_rows = adapter(which * (chips // 4), width_rows, gating_rows)
        up_rows = adapter(chips // 2 + which * (chips // 4), width_rows, gating_rows)
        gate = total[far, :, :half] + adapter_scale * contracted_rows(rank_rows, gate_rows)
        up = total[far, :, half:] + adapter_scale * contracted_rows(rank_rows, up_rows)
        active = (gate / (1.0 + jnp.exp(-gate)) * up).astype(bf16)
        hidden[:, far * half : (far + 1) * half] = active
        pieces = [
            pack(which * (chips // 2) + device // 2, device % 2, width_rows, hidden_rows)
            for device in range(chips)
        ]
        part = dot(active, jnp.concatenate(pieces, axis=0))
        low = part if low is None else low + part
    low_rank = jnp.where(in_rank, 0.0, low).astype(bf16)

    scales = []
    lane = lax.broadcasted_iota(jnp.int32, (block_rows, lane_count), 1)
    ours = (lane % chips == slots[me // 2]) & (lane < weight_terms * chips)
    for source in arrived:
        terms = jnp.where(ours, source[:, width:].astype(f32), 0.0)
        scales.append(jnp.sum(terms, axis=1, keepdims=True))

    for chip in range(chips):
        for core in range(2):
            begin = (2 * chip + core) * width_rows
            columns = slice(begin, begin + width_rows)
            result = dot(hidden[:, :half], near_down[0, :, columns])
            result = result + dot(hidden[:, half:], far_down[0, :, columns])
            result = result + adapter_scale * contracted_rows(low_rank, pack(chip, core, 0, width_rows))
            result = result.astype(bf16).astype(f32)
            for index in range(blocks):
                own = result[index * block_rows : (index + 1) * block_rows]
                part, first = divmod(begin, width // parts)
                out = outs[index * parts + part]
                out[:, first : first + width_rows] = (scales[index] * own).astype(bf16)


def rest_chunk(slots, rows, total, near_down, far_down, packs, parts):
    blocks, block_rows = len(rows), rows[0].shape[0]
    width, both = near_down.shape[2], 2 * near_down.shape[1]
    chips = packs[0].shape[0]
    return pl.pallas_call(
        partial(rest_kernel, blocks, chips),
        out_shape=[jax.ShapeDtypeStruct((block_rows, width // parts), bf16)] * (blocks * parts),
        in_specs=[in_smem] + [in_vmem] * (blocks + 5),
        out_specs=[in_vmem] * (blocks * parts),
        scratch_shapes=[
            pltpu.VMEM((blocks * block_rows, width), bf16),
            pltpu.VMEM((blocks * block_rows, both), bf16),
        ],
        compiler_params=pltpu.CompilerParams(vmem_limit_bytes=8 * 2**20),
        cost_estimate=small_cost,
        name="rest_chunk",
    )(slots, *rows, total, near_down, far_down, *packs)


def dense_per_device(
    tokens, routes, route_weights, slot_experts, gateup_base, down_base,
    entry_factor, gating_factor, hidden_factor, output_factor,
):
    chips = lax.axis_size("expert") // 2
    width_rows, rank = entry_factor.shape[1:]
    gating_rows = gating_factor.shape[1]
    order = ring_order(chips)
    size = width_rows + gating_rows
    devices = 2 * chips

    def keep(array):
        return pltpu.with_memory_space_constraint(array, pltpu.VMEM)

    def ahead(block):
        return lax.ppermute(block, "expert", hop_pairs(order, 1))

    def back(block):
        return lax.ppermute(block, "expert", hop_pairs(order, -1))

    def send_factors(block, send):
        pairs = hop_pairs(order, send)
        pairs += [(devices + here, devices + there) for here, there in hop_pairs(order, -send)]
        return lax.ppermute(block, ("groups", "expert"), pairs)

    sends = chips // 2 + 1
    shapes = [jax.ShapeDtypeStruct((size, 2 * rank), bf16)] * (sends - 1)
    shapes.append(jax.ShapeDtypeStruct((size // 2, 2 * rank), bf16))
    extended = jax.ShapeDtypeStruct((tokens.shape[0], tokens.shape[1] + lane_count), bf16)
    tokens, *packed = pl.pallas_call(
        partial(pack_kernel, chips),
        out_shape=[extended] + shapes,
        in_specs=[in_smem] + [in_vmem] * 7,
        out_specs=[in_vmem] * (sends + 1),
        scratch_shapes=[pltpu.VMEM((size, 2 * rank), bf16)],
        cost_estimate=small_cost,
        name="pack_factors",
    )(
        slot_experts, tokens, routes.T, route_weights.T,
        jnp.swapaxes(entry_factor, 1, 2), jnp.swapaxes(output_factor, 1, 2),
        jnp.swapaxes(gating_factor, 1, 2), hidden_factor,
    )
    rows = {0: tokens, 1: ahead(tokens)}
    got = [send_factors(packed[send], send) for send in range(1, sends)]

    rows[1], got, gateup, down = lax.optimization_barrier((rows[1], got, gateup_base, down_base))
    mine = pl.pallas_call(
        join_kernel,
        out_shape=jax.ShapeDtypeStruct((sum(part.shape[0] for part in got), 2 * rank), bf16),
        in_specs=[in_vmem] * (sends - 1),
        out_specs=in_vmem,
        compiler_params=pltpu.CompilerParams(vmem_limit_bytes=8 * 2**20),
        cost_estimate=small_cost,
        name="join_factors",
    )(*got)
    twins = lax.ppermute(mine, "groups", [(0, 1), (1, 0)])
    rows[7] = back(tokens)
    rows[2] = ahead(rows[1])
    far_gateup = partner(gateup, "expert", 0)
    near_gateup, near_down, ready = load_base(gateup, down)

    twins, rows[2], rows[7], ready, down = lax.optimization_barrier((twins, rows[2], rows[7], ready, down_base))
    near_pack = pl.pallas_call(
        partial(collect_kernel, chips),
        out_shape=jax.ShapeDtypeStruct((chips, size, 2 * rank), bf16),
        in_specs=[in_vmem] * 4,
        out_specs=in_vmem,
        compiler_params=pltpu.CompilerParams(vmem_limit_bytes=8 * 2**20),
        cost_estimate=small_cost,
        name="order_factors",
    )(packed[0], mine, twins, ready)
    far_pack = partner(near_pack, "expert", 0)
    far_down = partner(down, "expert", 0)
    gateups, downs = (near_gateup, keep(far_gateup)), (near_down, keep(far_down))
    packs = [keep(near_pack), keep(far_pack)]
    rows[6] = back(rows[7])
    rows[3] = ahead(rows[2])
    rows[5] = back(rows[6])
    rows[4] = ahead(rows[3])
    totals, terms = {}, {}

    def tied(blocks, after):
        return lax.optimization_barrier((blocks, after)) if after is not None else (blocks, after)

    def begin_chunk(members, after=None):
        blocks, after = tied([rows[hop] for hop in members], after)
        totals[members] = base_chunk(blocks, *gateups)
        return after

    def end_chunk(members, after=None):
        total, after = tied(totals[members], after)
        results = rest_chunk(slot_experts, [rows[hop] for hop in members], keep(total), *downs, packs, sum_parts)
        for index, hop in enumerate(members):
            terms[hop] = list(results[index * sum_parts : (index + 1) * sum_parts])
        return after

    begin_chunk(chunk_plan[0])
    end_chunk(chunk_plan[0])
    running = terms[1]
    running[-1] = begin_chunk(chunk_plan[1], running[-1])
    end_chunk(chunk_plan[1])
    for hop in range(2, chips + 1):
        running = [ahead(part) for part in running]
        if hop in begin_plan:
            running[-1] = begin_chunk(begin_plan[hop], running[-1])
        if hop in end_plan:
            running[-1] = end_chunk(end_plan[hop], running[-1])
        running = [
            (part.astype(f32) + term.astype(f32)).astype(bf16)
            for part, term in zip(running, terms[hop % chips])
        ]
    return jnp.concatenate(running, axis=1)


def program(*args):
    routes, entry_factor, tokens = args[1], args[6], args[0]
    experts, rank = entry_factor.shape[0], entry_factor.shape[2]
    every = routes.shape[1] == experts and lax.axis_size("expert") == 2 * experts
    every = every and lax.axis_size("groups") == 2 and experts == 8 and rank == 64 and tokens.shape[0] == rank
    return (dense_per_device if every else per_device)(*args)


def solution(mesh):
    in_specs = (
        P(("groups", "expert"), None),
        P(("groups", "expert"), None),
        P(("groups", "expert"), None),
        P(),
        P("expert", None, None),
        P("expert", None, None),
        P(None, "expert", None),
        P(None, "expert", None),
        P(None, "expert", None),
        P(None, "expert", None),
    )
    out_specs = P(("groups", "expert"), None)
    return jax.shard_map(
        program, mesh=mesh, in_specs=in_specs, out_specs=out_specs, check_vma=False
    )
```
